512 devices in a mesh: mem: 16 (over z_lo, core), lat: 32 (over z_hi, x, y).
Axes of the slice: x: 4, y: 4, z: 16 (z_hi: 2, z_lo: 8; z = z_hi * 8 + z_lo), core: 2. Of those that a mesh axis runs over, the one named last changes fastest.
Arguments:
- ensemble: float32 [1024, 256, 512], P('mem', 'lat'), may hold values from -6 to 6
- diffusivity: float32 [256, 512], P('lat'), may hold values from 0.02 to 0.2
- north_wind: float32 [256, 512], P('lat'), may hold values from -0.25 to 0.25
- observed_blocks: int32 [32, 16, 4], P('lat'), may hold values from 0 to 31
- eastern_average_flags: int32 [32, 16, 512], P('lat'), may hold values 0 or 1
- observed_values: float32 [32, 16, 512], P('lat', 'mem'), may hold values from -6 to 6
- observed_error: float32 [32, 16, 512], P('lat', 'mem'), may hold values from 0.5 to 4
Outputs:
- analysis: float32 [1024, 256, 512], P('mem', 'lat')
The draws below stay inside these ranges and needn't reach their ends.
Inputs may be any that keep to these rules, and one draw needn't show every extreme that they name: `observed_blocks`: block i covers a band's flattened cells i * 128 to (i + 1) * 128 - 1; blocks may repeat.
All inputs are finite; a program needn't handle non-finite values. No bound on the sum of `eastern_average_flags` on one device may be relied on, other than what follows from the above.
Results may differ from the reference program's by a relative error of at most 0.0003.
Values sent between devices are 32-bit elements; how exact they have to be, the bound alone decides.
A program may use at most 64 MiB of HBM per device.

```python
import math
import jax
import jax.numpy as jnp
from jax import lax

ACELLS = 256
LON = 512
OBS = 512
BLOCK = 128
NEWTON = 4
MEMBERS = 1024
PARALLEL_COUNT = 8
LAT = 256
BANDS = 32
PATCH_BAND = 16
NBLK = 4
BAND_BLOCKS = 32
N_MEM = 16
N_LAT = 32


def plant(array, own_key, least, high):
    dims = array.shape
    index_at = [jax.random.randint(jax.random.fold_in(own_key, axis), (), 0, dims[axis]) for axis in range(len(dims))]
    array = array.at[tuple(index_at)].set(least)
    longest = dims.index(max(dims))
    index_at[longest] = (index_at[longest] + 1) % dims[longest]
    return array.at[tuple(index_at)].set(high)


def steps_of(own_key, shape, cuts, least, top_value):
    def one(position, parts):
        heights = jax.random.uniform(jax.random.fold_in(jax.random.fold_in(own_key, 6), position), (parts,), jnp.float32, least / len(cuts), top_value / len(cuts))
        return jnp.repeat(jnp.exp(heights), shape[position] // parts).reshape((-1,) + (1,) * (len(shape) - position - 1))

    level = one(*cuts[0])
    for cut in cuts[1:]:
        level = level * one(*cut)
    return level


def normal_values(own_key, dims, deviation, limit, cuts=(), kind=jnp.bfloat16):
    entries = jax.random.normal(own_key, dims, jnp.float32) * deviation
    if len(cuts) > 0:
        entries = steps_of(own_key, dims, cuts, -0.22, 0.18) * entries
    return jnp.clip(entries, min=-limit, max=limit).astype(kind)


def setup_inputs(seed: int = 0) -> dict:
    key_of = jax.random.split(jax.random.key(seed), 8)
    return {
        "ensemble": normal_values(key_of[0], (MEMBERS, LAT, LON), 1.0, 6.0, ((0, 16), (1, 32)), jnp.float32),
        "diffusivity": jnp.clip(jnp.exp(math.log(0.2) - 2.3025851 * jax.random.uniform(key_of[1], (LAT, LON), jnp.float32) ** steps_of(key_of[1], (LAT, LON), ((0, 32),), -0.2, 0.2)), 0.02, 0.2),
        "north_wind": jnp.clip(jax.random.uniform(key_of[2], (LAT, LON), jnp.float32, -0.25, 0.25) * steps_of(key_of[2], (LAT, LON), ((0, 32),), -0.4, 0.0), -0.25, 0.25),
        "observed_blocks": plant(jax.random.randint(key_of[3], (BANDS, PATCH_BAND, NBLK), 0, BAND_BLOCKS), jax.random.fold_in(key_of[3], 1), 0, BAND_BLOCKS - 1).astype(jnp.int32),
        "eastern_average_flags": plant((jax.random.randint(key_of[4], (BANDS, PATCH_BAND, OBS), 0, 2) < 1).astype(jnp.int32), jax.random.fold_in(key_of[4], 1), 0, 1),
        "observed_values": normal_values(key_of[5], (BANDS, PATCH_BAND, OBS), 1.0, 6.0, ((0, 32), (1, 16)), jnp.float32),
        "observed_error": jnp.clip(jnp.exp(math.log(4.0) - 2.0794415 * jax.random.uniform(key_of[6], (BANDS, PATCH_BAND, OBS), jnp.float32) ** steps_of(key_of[6], (BANDS, PATCH_BAND, OBS), ((0, 32), (1, 16)), -0.2, 0.2)), 0.5, 4.0),
    }


ADVECTION = 0.1
HIGHEST = lax.Precision.HIGHEST


def advance(padded, diffusivity, north_wind):
    centre = padded[:, 1:-1, :]
    northern = padded[:, :-2, :]
    equatorward_side = padded[:, 2:, :]
    eastern = jnp.roll(centre, -1, axis=2)
    western_neighbour = jnp.roll(centre, 1, axis=2)
    return centre - ADVECTION * centre * (eastern - western_neighbour) - north_wind * (equatorward_side - northern) + diffusivity * (eastern + western_neighbour + northern + equatorward_side - 4.0 * centre)


def contract_first(left, right):
    return lax.dot_general(left, right, (((0,), (0,)), ((), ())), precision=HIGHEST, preferred_element_type=jnp.float32)


def patch_gain(cell_values, seen_values, values, errors):
    sample_states = cell_values.shape[0]
    cell_offset = cell_values - jnp.mean(cell_values, axis=0)
    seen_mean = jnp.mean(seen_values, axis=0)
    seen_offset = seen_values - seen_mean
    covariance = contract_first(seen_offset, seen_offset) / (sample_states - 1.0) + jnp.diag(errors)
    row_scale = jnp.sum(jnp.abs(covariance), axis=1)
    inverse = jnp.diag(1.0 / row_scale)
    for sweep in range(NEWTON):
        product = jnp.dot(covariance, inverse, precision=HIGHEST, preferred_element_type=jnp.float32)
        inverse = 2.0 * inverse - jnp.dot(inverse, product, precision=HIGHEST, preferred_element_type=jnp.float32)
    cross_cov = contract_first(cell_offset, seen_offset) / (sample_states - 1.0)
    gain = jnp.dot(cross_cov, inverse, precision=HIGHEST, preferred_element_type=jnp.float32)
    innovation = values - seen_mean
    return gain, innovation, seen_mean


def reference(ensemble, diffusivity, north_wind, observed_blocks, eastern_average_flags, observed_values, observed_error):
    sample_states, latitudes, meridian_total = ensemble.shape
    sample_partitions = ensemble.reshape(N_MEM, sample_states // N_MEM, latitudes, meridian_total)

    def background_state(variable_layers):
        for sweep in range(2):
            padded = jnp.pad(variable_layers, ((0, 0), (1, 1), (0, 0)))
            variable_layers = advance(padded, diffusivity, north_wind)
        return variable_layers

    variable_layers = lax.map(background_state, sample_partitions).reshape(sample_states, N_LAT, PARALLEL_COUNT * meridian_total)

    def patch(patch_index):
        band_index = patch_index // N_MEM
        segment_number = patch_index % N_MEM
        band_flat = lax.dynamic_index_in_dim(variable_layers, band_index, axis=1, keepdims=False)
        band_grid = band_flat.reshape(sample_states, PARALLEL_COUNT, meridian_total)
        block_tiles = band_flat.reshape(sample_states, -1, BLOCK)
        east_tiles = jnp.roll(band_grid, -1, axis=2).reshape(sample_states, -1, BLOCK)
        chosen = observed_blocks[band_index, segment_number].astype(jnp.int32)
        direct = jnp.take(block_tiles, chosen, axis=1).reshape(sample_states, OBS)
        shifted = jnp.take(east_tiles, chosen, axis=1).reshape(sample_states, OBS)
        lag_flags = eastern_average_flags[band_index, segment_number]
        seen_values = jnp.where(lag_flags[None, :] == 1, 0.5 * (direct + shifted), direct)
        cell_values = lax.dynamic_slice_in_dim(band_flat, (segment_number * ACELLS).astype(jnp.int32), ACELLS, axis=1)
        gain, innovation, seen_mean = patch_gain(cell_values, seen_values, observed_values[band_index, segment_number], observed_error[band_index, segment_number])
        weights = innovation[None, :] - 0.5 * (seen_values - seen_mean[None, :])
        update = lax.dot_general(weights, gain, (((1,), (1,)), ((), ())), precision=HIGHEST, preferred_element_type=jnp.float32)
        return cell_values + update

    result = lax.map(patch, jnp.arange(N_LAT * N_MEM, dtype=jnp.int32))
    result = result.reshape(N_LAT, N_MEM, sample_states, ACELLS).transpose(2, 0, 1, 3)
    return result.reshape(sample_states, latitudes, meridian_total)
```

```python
import jax
import jax.numpy as jnp
from jax import lax
from jax.experimental import pallas as pl
from jax.experimental.pallas import tpu as pltpu
from jax.sharding import PartitionSpec as P

MESH = pl.DeviceIdType.MESH
BOTH = ("mem", "lat")
ADVECTION = 0.1
CHUNKS = 4
MEMBERS = 64
ROWS = MEMBERS // CHUNKS
PREC = lax.Precision.HIGH


def m8(v):
    return (v + 16) % 8


def device(z, c, h, s, w):
    return (z * 2 + c, h * 16 + (w // 2) * 4 + s * 2 + w % 2)


def place():
    m, l = lax.axis_index("mem"), lax.axis_index("lat")
    return m // 2, m % 2, l // 16, (l % 4) // 2, ((l // 4) % 4) * 2 + l % 2


def to_plane():
    pairs = []
    for m in range(16):
        for l in range(32):
            z, c, h, s, w = m // 2, m % 2, l // 16, (l % 4) // 2, ((l // 4) % 4) * 2 + l % 2
            a, b = device(w, c, h, s, m8(w - z + 4 * c))
            pairs.append((m * 32 + l, a * 32 + b))
    return pairs


def enter(peers, others):
    barrier = pltpu.get_barrier_semaphore()

    @pl.loop(1, 16)
    def _(i):
        pl.semaphore_signal(barrier, inc=1, device_id=peers(i), device_id_type=MESH)

    (first, second), there = others

    @pl.when(there)
    def _():
        pl.semaphore_signal(barrier, inc=1, device_id=first, device_id_type=MESH)
        pl.semaphore_signal(barrier, inc=1, device_id=second, device_id_type=MESH)
        pl.semaphore_wait(barrier, 17)

    @pl.when(jnp.logical_not(there))
    def _():
        pl.semaphore_wait(barrier, 15)


class Move:
    def __init__(self, source, target, send, recv, where, away):
        self.away, self.home = away, jnp.logical_not(away)
        self.remote = pltpu.make_async_remote_copy(
            source, target, send, recv, device_id=where, device_id_type=MESH
        )
        self.local = pltpu.make_async_copy(source, target, recv)

    def start(self):
        pl.when(self.away)(self.remote.start)
        pl.when(self.home)(self.local.start)

    def wait_recv(self):
        pl.when(self.away)(self.remote.wait_recv)
        pl.when(self.home)(self.local.wait)

    def wait_send(self):
        pl.when(self.away)(self.remote.wait_send)


def gather_kernel(blocks, nexts, flags, field, out, *scratch):
    near, far, stage = scratch[:CHUNKS], scratch[CHUNKS : 2 * CHUNKS], scratch[2 * CHUNKS : 3 * CHUNKS]
    spread_send, spread_recv, hop_send, hop_recv, send, recv = scratch[3 * CHUNKS :]
    z, c, h, s, w = place()
    mine = w * 2 + c
    patch = m8(z - w + 4 * c) * 2 + c

    def peer(i):
        k = (mine + i) % 16
        return k, device(z, k % 2, h, s, k // 2)

    hop_to, hop_from = device(m8(w + z - 4 * c), c, h, s, w), device(m8(z - w + 4 * c), c, h, s, w)
    hops = m8(w - 4 * c) != 0
    enter(lambda i: peer(i)[1], ((hop_to, hop_from), hops))

    spread_to = device(z, c, h, s, m8(w - z + 4 * c))
    spreads = m8(4 * c - z) != 0
    spread = [
        Move(field.at[:, pl.ds(i * ROWS, ROWS)], near[i], spread_send.at[i], spread_recv.at[i], spread_to, spreads)
        for i in range(CHUNKS)
    ]
    hop = [Move(near[i], far[i], hop_send.at[i], hop_recv.at[i], hop_to, hops) for i in range(CHUNKS)]

    def piece(i, off):
        k, where = peer(off)
        wanted = m8(z - k // 2 + 4 * (k % 2)) * 2 + k % 2
        return pltpu.make_async_remote_copy(
            stage[i].at[wanted],
            out.at[mine, pl.ds(i * ROWS, ROWS)],
            send.at[i, off],
            recv.at[i, off],
            device_id=where,
            device_id_type=MESH,
        )

    def own(i):
        return pltpu.make_async_copy(stage[i].at[patch], out.at[mine, pl.ds(i * ROWS, ROWS)], recv.at[i, 0])

    first_lane = lax.broadcasted_iota(jnp.int32, (ROWS, 128), 1) == 0

    def observe(i):
        hop[i].wait_recv()
        tiles, put = far[i], stage[i]

        @pl.loop(0, 16)
        def _(p):
            for t in range(2):
                put[p, :, t * 128 : (t + 1) * 128] = tiles[2 * p + t]
            for j in range(4):
                direct = tiles[blocks[p * 4 + j]]
                beside = jnp.where(first_lane, tiles[nexts[p * 4 + j]], direct)
                east = pltpu.roll(beside, 127, 1)
                seen = jnp.where(flags[p * 4 + j] == 1, 0.5 * (direct + east), direct)
                put[p, :, 256 + j * 128 : 384 + j * 128] = seen

        @pl.loop(1, 16)
        def _(off):
            piece(i, off).start()

        own(i).start()

    for i in range(CHUNKS):
        spread[i].start()
    for i in range(CHUNKS):
        spread[i].wait_recv()
        hop[i].start()
        if i > 0:
            observe(i - 1)
    observe(CHUNKS - 1)
    for i in range(CHUNKS):

        @pl.loop(1, 16)
        def _(off):
            piece(i, off).wait()

        own(i).wait()
        spread[i].wait_send()
        hop[i].wait_send()


def gather(field, blocks, nexts, flags):
    chunk = pltpu.VMEM((32, ROWS, 128), jnp.float32)
    dma = pltpu.SemaphoreType.DMA
    vmem, smem = pl.BlockSpec(memory_space=pltpu.VMEM), pl.BlockSpec(memory_space=pltpu.SMEM)
    return pl.pallas_call(
        gather_kernel,
        out_shape=jax.ShapeDtypeStruct((16, MEMBERS, 768), jnp.float32),
        in_specs=[smem, smem, vmem, vmem],
        out_specs=vmem,
        scratch_shapes=[chunk] * (2 * CHUNKS)
        + [pltpu.VMEM((16, ROWS, 768), jnp.float32)] * CHUNKS
        + [dma((CHUNKS,))] * 4
        + [dma((CHUNKS, 16))] * 2,
        compiler_params=pltpu.CompilerParams(
            collective_id=0, has_side_effects=True, vmem_limit_bytes=40 * 2**20
        ),
        name="gather",
    )(blocks, nexts, flags, field)


def scatter_kernel(cells, out, *scratch):
    held = scratch[:CHUNKS]
    home_send, home_recv, send, recv = scratch[CHUNKS:]
    z, c, h, s, w = place()
    mine = w * 2 + c
    patch = m8(z - w + 4 * c) * 2 + c

    def peer(i):
        k = (mine + i) % 16
        return k, device(z, k % 2, h, s, k // 2)

    home, guest = device(m8(z - w + 4 * c), c, h, s, z), device(w, c, h, s, m8(w - z + 4 * c))
    away = jnp.logical_or(w != z, m8(z - w + 4 * c) != z)
    enter(lambda i: peer(i)[1], ((home, guest), away))

    def piece(i, off):
        k, where = peer(off)
        return pltpu.make_async_remote_copy(
            cells.at[k, pl.ds(i * ROWS, ROWS)],
            held[i].at[patch],
            send.at[i, off],
            recv.at[i, off],
            device_id=where,
            device_id_type=MESH,
        )

    def own(i):
        return pltpu.make_async_copy(cells.at[mine, pl.ds(i * ROWS, ROWS)], held[i].at[patch], recv.at[i, 0])

    back = [
        Move(held[i], out.at[:, pl.ds(i * ROWS, ROWS)], home_send.at[i], home_recv.at[i], home, away)
        for i in range(CHUNKS)
    ]
    for i in range(CHUNKS):

        @pl.loop(1, 16)
        def _(off):
            piece(i, off).start()

        own(i).start()
    for i in range(CHUNKS):

        @pl.loop(1, 16)
        def _(off):
            piece(i, off).wait()

        own(i).wait()
        back[i].start()
    for i in range(CHUNKS):
        back[i].wait_recv()
        back[i].wait_send()


def scatter(cells):
    dma = pltpu.SemaphoreType.DMA
    vmem = pl.BlockSpec(memory_space=pltpu.VMEM)
    return pl.pallas_call(
        scatter_kernel,
        out_shape=jax.ShapeDtypeStruct((16, MEMBERS, 256), jnp.float32),
        in_specs=[vmem],
        out_specs=vmem,
        scratch_shapes=[pltpu.VMEM((16, ROWS, 256), jnp.float32)] * CHUNKS
        + [dma((CHUNKS,))] * 2
        + [dma((CHUNKS, 16))] * 2,
        compiler_params=pltpu.CompilerParams(
            collective_id=1, has_side_effects=True, vmem_limit_bytes=40 * 2**20
        ),
        name="scatter",
    )(cells)


def advance(padded, diffusivity, north_wind):
    centre, northern, southern = padded[1:-1], padded[:-2], padded[2:]
    eastern = jnp.roll(centre, -1, axis=2)
    western = jnp.roll(centre, 1, axis=2)
    return (
        centre
        - ADVECTION * centre * (eastern - western)
        - north_wind * (southern - northern)
        + diffusivity * (eastern + western + northern + southern - 4.0 * centre)
    )


def forecast(ensemble, diffusivity, north_wind):
    bands = lax.axis_size("lat")
    ahead = [(i, i + 1) for i in range(bands - 1)]
    behind = [(i + 1, i) for i in range(bands - 1)]
    field = ensemble.transpose(1, 0, 2)
    terms = jnp.stack([diffusivity, north_wind], axis=1)

    def edge(first, last, field_rows, term_rows):
        del first, last
        return jnp.concatenate([field_rows.reshape(-1, 512), term_rows.reshape(-1, 512)])

    count = 2 * field.shape[1]
    low = lax.ppermute(edge(0, 0, field[-2:], terms[-1:]), "lat", ahead)
    high = lax.ppermute(edge(0, 0, field[:2], terms[:1]), "lat", behind)
    padded = jnp.concatenate(
        [low[:count].reshape(2, -1, 512), field, high[:count].reshape(2, -1, 512)]
    )
    terms = jnp.concatenate([low[count:][None], terms, high[count:][None]])
    band = lax.axis_index("lat")
    row = lax.broadcasted_iota(jnp.int32, (10, 1, 1), 0)
    inside = jnp.logical_and(
        jnp.logical_or(row > 0, band > 0), jnp.logical_or(row < 9, band < bands - 1)
    )
    once = advance(padded, terms[:, 0:1], terms[:, 1:2])
    once = jnp.where(inside, once, 0.0)
    return advance(once, terms[1:-1, 0:1], terms[1:-1, 1:2])


def dot(left, right):
    return jnp.dot(left, right, precision=PREC, preferred_element_type=jnp.float32)


def analyse(states, values, errors):
    count = states.shape[0]
    mean = jnp.mean(states, axis=0)
    offset = states - mean
    seen_offset = offset[:, 256:]
    products = lax.dot_general(
        offset, seen_offset, (((0,), (0,)), ((), ())), precision=PREC, preferred_element_type=jnp.float32
    ) / (count - 1.0)
    covariance = products[256:] + jnp.diag(errors)
    scale = lax.rsqrt(jnp.sum(jnp.abs(covariance), axis=1))
    power = jnp.eye(512, dtype=jnp.float32) - covariance * scale[:, None] * scale[None, :]
    gain = products[:256] * scale[None, :]
    for step in range(4):
        gain = gain + dot(gain, power)
        if step < 3:
            power = dot(power, power)
    gain = gain * scale[None, :]
    weights = (values - mean[256:])[None, :] - 0.5 * seen_offset
    update = lax.dot_general(
        weights, gain, (((1,), (1,)), ((), ())), precision=PREC, preferred_element_type=jnp.float32
    )
    return states[:, :256] + update


def body(ensemble, diffusivity, north_wind, observed_blocks, eastern_average_flags, observed_values, observed_error):
    small = jnp.concatenate(
        [
            eastern_average_flags[0].astype(jnp.float32),
            observed_values[0],
            observed_error[0],
            jnp.pad(observed_blocks[0].reshape(1, 64).astype(jnp.float32), ((0, 0), (0, 448))),
        ]
    )
    small = lax.ppermute(small, BOTH, to_plane())
    flags = small[:16].astype(jnp.int32).reshape(64, 1, 128)
    values, errors = small[16], small[17]
    blocks = small[18, :64].astype(jnp.int32)
    nexts = blocks - blocks % 4 + (blocks + 1) % 4
    field = forecast(ensemble, diffusivity, north_wind)
    field = field.reshape(8, MEMBERS, 4, 128).transpose(0, 2, 1, 3).reshape(32, MEMBERS, 128)
    states = gather(field, blocks, nexts, flags).reshape(16 * MEMBERS, 768)
    cells = analyse(states, values, errors).reshape(16, MEMBERS, 256)
    out = scatter(cells)
    return out.reshape(8, 2, MEMBERS, 256).transpose(2, 0, 1, 3).reshape(MEMBERS, 8, 512)


def solution(mesh):
    return jax.shard_map(
        body,
        mesh=mesh,
        in_specs=(
            P("mem", "lat", None),
            P("lat", None),
            P("lat", None),
            P("lat", None, None),
            P("lat", None, None),
            P("lat", "mem", None),
            P("lat", "mem", None),
        ),
        out_specs=P("mem", "lat", None),
        check_vma=False,
    )
```

```python
import jax
import jax.numpy as jnp
from jax import lax
from jax.experimental import pallas as pl
from jax.experimental.pallas import tpu as pltpu
from jax.sharding import PartitionSpec as P

MESH = pl.DeviceIdType.MESH
ADVECTION = 0.1
CHUNKS = 4
MEMBERS = 64
ROWS = MEMBERS // CHUNKS
PREC = lax.Precision.HIGH


def m8(v):
    return (v + 16) % 8


def device(z, c, h, s, w):
    return (z * 2 + c, h * 16 + (w // 2) * 4 + s * 2 + w % 2)


def place():
    m, l = lax.axis_index("mem"), lax.axis_index("lat")
    return m // 2, m % 2, l // 16, (l % 4) // 2, ((l // 4) % 4) * 2 + l % 2


def enter(peers, sources, targets):
    barrier = pltpu.get_barrier_semaphore()

    @pl.loop(1, 16)
    def _(i):
        pl.semaphore_signal(barrier, inc=1, device_id=peers(i), device_id_type=MESH)

    for there, source in sources:

        @pl.when(there)
        def _():
            pl.semaphore_signal(barrier, inc=1, device_id=source, device_id_type=MESH)

    count = 15
    for there in targets:
        count = count + jnp.where(there, 1, 0)
    pl.semaphore_wait(barrier, count)


class Move:
    def __init__(self, source, target, send, recv, where, away):
        self.away, self.home = away, jnp.logical_not(away)
        self.remote = pltpu.make_async_remote_copy(
            source, target, send, recv, device_id=where, device_id_type=MESH
        )
        self.local = pltpu.make_async_copy(source, target, recv)

    def start(self):
        pl.when(self.away)(self.remote.start)
        pl.when(self.home)(self.local.start)

    def wait_recv(self):
        pl.when(self.away)(self.remote.wait_recv)
        pl.when(self.home)(self.local.wait)

    def wait_send(self):
        pl.when(self.away)(self.remote.wait_send)


def advance(centre, north, south, terms, first_lane, last_lane):
    out = []
    for q in range(4):
        mid = centre[q]
        east = pltpu.roll(jnp.where(first_lane, centre[(q + 1) % 4], mid), 127, 1)
        west = pltpu.roll(jnp.where(last_lane, centre[(q + 3) % 4], mid), 1, 1)
        out.append(
            mid
            - ADVECTION * mid * (east - west)
            - terms[4 + q] * (south[q] - north[q])
            + terms[q] * (east + west + north[q] + south[q] - 4.0 * mid)
        )
    return out


def gather_kernel(field, terms, extra, where, out, extra_out, *scratch):
    n = CHUNKS
    low, high, relay, cast, near, far, stage = (scratch[n * k : n * (k + 1)] for k in range(7))
    term_edges, extra_near, where_near, where_far, blocks, once = scratch[7 * n : 7 * n + 6]
    sems = scratch[7 * n + 6 :]
    up_send, down_send, low_recv, high_recv, relay_send, relay_recv = sems[:6]
    spread_send, spread_recv, hop_send, hop_recv, send, recv, table = sems[6:]
    mem, lat = lax.axis_index("mem"), lax.axis_index("lat")
    z, c, h, s, w = place()
    mine = w * 2 + c
    group = m8(z - w + 4 * c)
    patch = group * 2 + c

    def peer(i):
        k = (mine + i) % 16
        return k, device(z, k % 2, h, s, k // 2)

    hops = m8(w - 4 * c) != 0
    hop_to, hop_from = device(m8(w + z - 4 * c), c, h, s, w), device(group, c, h, s, w)
    up_far, down_far = (lat == 15) & (mem != 15), (lat == 16) & (mem != 0)
    up_near, down_near = (lat < 31) & jnp.logical_not(up_far), (lat > 0) & jnp.logical_not(down_far)
    relays_up, relays_down = (lat == mem) & (lat != 15), (lat == mem + 16) & (lat != 16)
    relays = relays_up | relays_down
    low_from = (mem, jnp.where((lat == 16) & (mem != 15), mem, jnp.maximum(lat - 1, 0)))
    high_from = (mem, jnp.where((lat == 15) & (mem != 0), mem + 16, jnp.minimum(lat + 1, 31)))
    relay_from = (mem, jnp.where(relays_up, 15, 16))
    enter(
        lambda i: peer(i)[1],
        ((hops, hop_from), (lat > 0, low_from), (lat < 31, high_from), (relays, relay_from)),
        (hops, lat < 31, lat > 0, relays),
    )

    def remote(source, target, sends, recvs, i, to):
        return pltpu.make_async_remote_copy(
            source, target, sends.at[i], recvs.at[i], device_id=to, device_id_type=MESH
        )

    class Edge:
        def __init__(self, i):
            if i == 0:
                first, last, bottom, top = terms.at[0], terms.at[7], term_edges.at[0], term_edges.at[1]
                held = term_edges.at[2]
            else:
                rows = pl.ds((i - 1) * ROWS, ROWS)
                first, last = field.at[pl.ds(0, 8), rows], field.at[pl.ds(24, 8), rows]
                bottom, top, held = low[i - 1], high[i - 1], relay[i - 1]
            above, below = (mem, jnp.minimum(lat + 1, 31)), (mem, jnp.maximum(lat - 1, 0))
            self.bottom, self.top = bottom, top
            self.ups = (
                (up_near, remote(last, bottom, up_send, low_recv, i, above)),
                (up_far, remote(last, held, up_send, relay_recv, i, (mem, mem))),
            )
            self.downs = (
                (down_near, remote(first, top, down_send, high_recv, i, below)),
                (down_far, remote(first, held, down_send, relay_recv, i, (mem, mem + 16))),
            )
            self.passes = (
                (relays_up, remote(held, bottom, relay_send, low_recv, i, (mem, 16))),
                (relays_down, remote(held, top, relay_send, high_recv, i, (mem, 15))),
            )

        def start(self):
            for there, copy in self.ups + self.downs:
                pl.when(there)(copy.start)

            @pl.when(lat == 0)
            def _():
                self.bottom[...] = jnp.zeros(self.bottom.shape, jnp.float32)

            @pl.when(lat == 31)
            def _():
                self.top[...] = jnp.zeros(self.top.shape, jnp.float32)

        def forward(self):
            for (there, copy), (_, arriving) in zip(self.passes, (self.ups[1], self.downs[1])):

                @pl.when(there)
                def _():
                    arriving.wait_recv()
                    copy.start()

        def wait(self):
            pl.when(lat > 0)(self.ups[0][1].wait_recv)
            pl.when(lat < 31)(self.downs[0][1].wait_recv)

        def end(self):
            for there, copy in self.ups + self.downs + self.passes:
                pl.when(there)(copy.wait_send)

    spread_to = device(z, c, h, s, m8(w - z + 4 * c))
    spreads = m8(4 * c - z) != 0
    parts = list(zip(cast, near, far)) + [(extra, extra_near, extra_out), (where, where_near, where_far)]
    spread = [Move(a, b, spread_send.at[i], spread_recv.at[i], spread_to, spreads) for i, (a, b, _) in enumerate(parts)]
    hop = [Move(b, d, hop_send.at[i], hop_recv.at[i], hop_to, hops) for i, (_, b, d) in enumerate(parts)]

    def piece(i, off):
        k, there = peer(off)
        wanted = m8(z - k // 2 + 4 * (k % 2)) * 2 + k % 2
        return pltpu.make_async_remote_copy(
            stage[i].at[wanted],
            out.at[mine, pl.ds(i * ROWS, ROWS)],
            send.at[i, off],
            recv.at[i, off],
            device_id=there,
            device_id_type=MESH,
        )

    def own(i):
        return pltpu.make_async_copy(stage[i].at[patch], out.at[mine, pl.ds(i * ROWS, ROWS)], recv.at[i, 0])

    lane = lax.broadcasted_iota(jnp.int32, (ROWS, 128), 1)
    first_lane, last_lane = lane == 0, lane == 127

    def forecast(i):
        rows = slice(i * ROWS, (i + 1) * ROWS)

        def before(k):
            if isinstance(k, int) and k < 2:
                return [low[i][4 * k + q] for q in range(4)]
            if isinstance(k, int) and k > 9:
                return [high[i][4 * k - 40 + q] for q in range(4)]
            return [field[4 * k - 8 + q, rows] for q in range(4)]

        def middle(k):
            return [once[4 * k + q] for q in range(4)]

        def first(r):
            if isinstance(r, int) and r == 0:
                own_terms = [term_edges[0, q : q + 1] for q in range(8)]
            elif isinstance(r, int) and r == 9:
                own_terms = [term_edges[1, q : q + 1] for q in range(8)]
            else:
                own_terms = [terms[r - 1, q : q + 1] for q in range(8)]
            new = advance(before(r + 1), before(r), before(r + 2), own_terms, first_lane, last_lane)
            for q in range(4):
                once[4 * r + q] = new[q]

        for r in (0, 1, 8, 9):
            first(r)
        pl.loop(2, 8)(first)

        @pl.loop(0, 8)
        def _(r):
            own_terms = [terms[r, q : q + 1] for q in range(8)]
            new = advance(middle(r + 1), middle(r), middle(r + 2), own_terms, first_lane, last_lane)
            for q in range(4):
                cast[i][4 * r + q] = new[q]

    def observe(i):
        tiles, put = far[i], stage[i]

        @pl.loop(0, 8)
        def _(half):
            for p in range(2):
                for t in range(2):
                    put[2 * half + p, :, t * 128 : (t + 1) * 128] = tiles[4 * half + 2 * p + t]
                for j in range(4):
                    at = half * 8 + p * 4 + j
                    direct = tiles[blocks[0, at]]
                    beside = jnp.where(first_lane, tiles[blocks[1, at]], direct)
                    east = pltpu.roll(beside, 127, 1)
                    flag = extra_out[half, p * 4 + j : p * 4 + j + 1]
                    seen = jnp.where(flag == 1.0, 0.5 * (direct + east), direct)
                    put[2 * half + p, :, 256 + j * 128 : 384 + j * 128] = seen

        @pl.loop(1, 16)
        def _(off):
            piece(i, off).start()

        own(i).start()

    edges = [Edge(i) for i in range(n + 1)]
    for edge in edges:
        edge.start()
    spread[n].start()
    spread[n + 1].start()
    for i, edge in enumerate(edges):
        edge.forward()
        edge.wait()
        if i > 0:
            forecast(i - 1)
            spread[i - 1].start()
        if i == 2:
            for k in (n, n + 1, 0):
                spread[k].wait_recv()
                hop[k].start()
    for i in range(n):
        if i + 1 < n:
            spread[i + 1].wait_recv()
            hop[i + 1].start()
        if i == 0:
            hop[n].wait_recv()
            hop[n + 1].wait_recv()
            read = pltpu.make_async_copy(where_far, blocks, table)
            read.start()
            read.wait()
        hop[i].wait_recv()
        observe(i)
    for edge in edges:
        edge.end()
    for move in spread + hop:
        move.wait_send()
    for i in range(n):

        @pl.loop(1, 16)
        def _(off):
            piece(i, off).wait()

        own(i).wait()


def gather(field, terms, extra, where):
    def buffer(*shape):
        return pltpu.VMEM(shape, jnp.float32)

    n = CHUNKS
    dma, table = pltpu.SemaphoreType.DMA, pltpu.VMEM((8, 128), jnp.int32)
    vmem = pl.BlockSpec(memory_space=pltpu.VMEM)
    return pl.pallas_call(
        gather_kernel,
        out_shape=(
            jax.ShapeDtypeStruct((16, MEMBERS, 768), jnp.float32),
            jax.ShapeDtypeStruct((9, 8, 128), jnp.float32),
        ),
        in_specs=[vmem] * 4,
        out_specs=(vmem, vmem),
        scratch_shapes=[buffer(8, ROWS, 128)] * (3 * n)
        + [buffer(32, ROWS, 128)] * (3 * n)
        + [buffer(16, ROWS, 768)] * n
        + [buffer(3, 8, 128), buffer(9, 8, 128), table, table]
        + [pltpu.SMEM((8, 128), jnp.int32), buffer(40, ROWS, 128)]
        + [dma((n + 1,))] * 6
        + [dma((n + 2,))] * 4
        + [dma((n, 16))] * 2
        + [dma],
        compiler_params=pltpu.CompilerParams(
            collective_id=0, has_side_effects=True, vmem_limit_bytes=40 * 2**20
        ),
        name="gather",
    )(field, terms, extra, where)


def scatter_kernel(cells, out, *scratch):
    held = scratch[:CHUNKS]
    home_send, home_recv, send, recv = scratch[CHUNKS:]
    z, c, h, s, w = place()
    mine = w * 2 + c
    group = m8(z - w + 4 * c)
    patch = group * 2 + c

    def peer(i):
        k = (mine + i) % 16
        return k, device(z, k % 2, h, s, k // 2)

    home, guest = device(group, c, h, s, z), device(w, c, h, s, m8(w - z + 4 * c))
    away = jnp.logical_or(w != z, group != z)
    enter(lambda i: peer(i)[1], ((away, guest),), (away,))

    def piece(i, off):
        k, where = peer(off)
        return pltpu.make_async_remote_copy(
            cells.at[k, pl.ds(i * ROWS, ROWS)],
            held[i].at[patch],
            send.at[i, off],
            recv.at[i, off],
            device_id=where,
            device_id_type=MESH,
        )

    def own(i):
        return pltpu.make_async_copy(cells.at[mine, pl.ds(i * ROWS, ROWS)], held[i].at[patch], recv.at[i, 0])

    def start(i):
        @pl.loop(1, 16)
        def _(off):
            piece(i, off).start()

        own(i).start()

    back = [
        Move(held[i], out.at[:, pl.ds(i * ROWS, ROWS)], home_send.at[i], home_recv.at[i], home, away)
        for i in range(CHUNKS)
    ]
    start(0)
    for i in range(CHUNKS):

        @pl.loop(1, 16)
        def _(off):
            piece(i, off).wait_recv()

        own(i).wait()
        back[i].start()
        if i + 1 < CHUNKS:
            start(i + 1)
    for i in range(CHUNKS):
        back[i].wait_recv()
        back[i].wait_send()

        @pl.loop(1, 16)
        def _(off):
            piece(i, off).wait_send()


def scatter(cells):
    dma = pltpu.SemaphoreType.DMA
    vmem = pl.BlockSpec(memory_space=pltpu.VMEM)
    return pl.pallas_call(
        scatter_kernel,
        out_shape=jax.ShapeDtypeStruct((16, MEMBERS, 256), jnp.float32),
        in_specs=[vmem],
        out_specs=vmem,
        scratch_shapes=[pltpu.VMEM((16, ROWS, 256), jnp.float32)] * CHUNKS
        + [dma((CHUNKS,))] * 2
        + [dma((CHUNKS, 16))] * 2,
        compiler_params=pltpu.CompilerParams(
            collective_id=1, has_side_effects=True, vmem_limit_bytes=40 * 2**20
        ),
        name="scatter",
    )(cells)


def dot(left, right):
    return jnp.dot(left, right, precision=PREC, preferred_element_type=jnp.float32)


def analyse(states, values, errors):
    count = states.shape[0]
    mean = jnp.mean(states, axis=0)
    offset = states - mean
    seen_offset = offset[:, 256:]
    products = lax.dot_general(
        offset, seen_offset, (((0,), (0,)), ((), ())), precision=PREC, preferred_element_type=jnp.float32
    ) / (count - 1.0)
    covariance = products[256:] + jnp.diag(errors)
    scale = lax.rsqrt(jnp.sum(jnp.abs(covariance), axis=1))
    power = jnp.eye(512, dtype=jnp.float32) - covariance * scale[:, None] * scale[None, :]
    gain = products[:256] * scale[None, :]
    for step in range(4):
        gain = gain + dot(gain, power)
        if step < 3:
            power = dot(power, power)
    gain = gain * scale[None, :]
    weights = (values - mean[256:])[None, :] - 0.5 * seen_offset
    update = lax.dot_general(
        weights, gain, (((1,), (1,)), ((), ())), precision=PREC, preferred_element_type=jnp.float32
    )
    return states[:, :256] + update


def body(ensemble, diffusivity, north_wind, observed_blocks, eastern_average_flags, observed_values, observed_error):
    terms = jnp.concatenate([diffusivity.reshape(8, 4, 128), north_wind.reshape(8, 4, 128)], axis=1)
    extra = jnp.concatenate(
        [
            eastern_average_flags[0].astype(jnp.float32).reshape(8, 8, 128),
            jnp.concatenate([observed_values.reshape(1, 4, 128), observed_error.reshape(1, 4, 128)], axis=1),
        ]
    )
    blocks = observed_blocks[0].reshape(1, 64)
    nexts = blocks - blocks % 4 + (blocks + 1) % 4
    where = jnp.pad(jnp.concatenate([blocks, nexts]), ((0, 6), (0, 64)))
    field = ensemble.reshape(MEMBERS, 8, 4, 128).transpose(1, 2, 0, 3).reshape(32, MEMBERS, 128)
    states, extra = gather(field, terms, extra, where)
    states = states.reshape(16 * MEMBERS, 768)
    values, errors = extra[8, :4].reshape(512), extra[8, 4:].reshape(512)
    cells = analyse(states, values, errors).reshape(16, MEMBERS, 256)
    out = scatter(cells)
    return out.reshape(8, 2, MEMBERS, 256).transpose(2, 0, 1, 3).reshape(MEMBERS, 8, 512)


def solution(mesh):
    return jax.shard_map(
        body,
        mesh=mesh,
        in_specs=(
            P("mem", "lat", None),
            P("lat", None),
            P("lat", None),
            P("lat", None, None),
            P("lat", None, None),
            P("lat", "mem", None),
            P("lat", "mem", None),
        ),
        out_specs=P("mem", "lat", None),
        check_vma=False,
    )
```

```python
import jax
import jax.numpy as jnp
from jax import lax
from jax.experimental import pallas as pl
from jax.experimental.pallas import tpu as pltpu
from jax.sharding import PartitionSpec as P

MESH = pl.DeviceIdType.MESH
ADVECTION = 0.1
MEMBERS = 64
OUT = (16, 16, 16, 16)
BACK = (16, 16, 16, 16)
PREC = lax.Precision.HIGH

PEERS = (
    (0, 1, 0), (1, 0, 0), (3, 0, 0), (2, 1, 0), (1, 1, 0), (3, 1, 0), (2, 0, 0), (0, 1, 1),
    (1, 0, 1), (3, 0, 1), (2, 1, 1), (0, 0, 1), (1, 1, 1), (3, 1, 1), (2, 0, 1),
)

SPIN, SIDE = (7, 3, 5), 5


def both(*values):
    return sum(sum(v // 2**i % 2 for v in values) % 2 * 2**i for i in range(3))


def mix(rows, v):
    return sum(sum(v // 2**j % 2 for j in range(3) if rows[i] // 2**j % 2) % 2 * 2**i for i in range(3))


UNSPIN = next(
    rows
    for rows in ((i, j, k) for i in range(8) for j in range(8) for k in range(8))
    if all(mix(rows, mix(SPIN, v)) == v for v in range(8))
)


def lane(w, z, c):
    return both(w, mix(SPIN, z), SIDE * c)


def member(z, w, c):
    return mix(UNSPIN, both(z, w, SIDE * c))


def device(z, c, h, s, w):
    return (z * 2 + c, h * 16 + (w // 2) * 4 + s * 2 + w % 2)


def place():
    m, l = lax.axis_index("mem"), lax.axis_index("lat")
    return m // 2, m % 2, l // 16, (l % 4) // 2, ((l // 4) % 4) * 2 + l % 2


def enter(peers, sources, targets):
    barrier = pltpu.get_barrier_semaphore()

    for i in range(1, 16):
        pl.semaphore_signal(barrier, inc=1, device_id=peers(i), device_id_type=MESH)

    for there, source in sources:

        @pl.when(there)
        def _():
            pl.semaphore_signal(barrier, inc=1, device_id=source, device_id_type=MESH)

    count = 15
    for there in targets:
        count = count + jnp.where(there, 1, 0)
    pl.semaphore_wait(barrier, count)


def rows(sizes, i):
    return pl.ds(sum(sizes[:i]), sizes[i])


class Move:
    def __init__(self, source, target, send, recv, where, away):
        self.away, self.home = away, jnp.logical_not(away)
        self.remote = pltpu.make_async_remote_copy(
            source, target, send, recv, device_id=where, device_id_type=MESH
        )
        self.local = pltpu.make_async_copy(source, target, recv)

    def start(self):
        pl.when(self.away)(self.remote.start)
        pl.when(self.home)(self.local.start)

    def wait_recv(self):
        pl.when(self.away)(self.remote.wait_recv)
        pl.when(self.home)(self.local.wait)

    def wait_send(self):
        pl.when(self.away)(self.remote.wait_send)


def advance(centre, north, south, terms, first_lane, last_lane):
    out = []
    for q in range(4):
        mid = centre[q]
        east = pltpu.roll(jnp.where(first_lane, centre[(q + 1) % 4], mid), 127, 1)
        west = pltpu.roll(jnp.where(last_lane, centre[(q + 3) % 4], mid), 1, 1)
        out.append(
            mid
            - ADVECTION * mid * (east - west)
            - terms[4 + q] * (south[q] - north[q])
            + terms[q] * (east + west + north[q] + south[q] - 4.0 * mid)
        )
    return out


def gather_kernel(field, diffusivity, north_wind, flags, values, errors, where, out, *rest):
    n = len(OUT)
    values_out, errors_out, *scratch = rest
    low, high, relay, cast, near, far, stage = (scratch[n * k : n * (k + 1)] for k in range(7))
    diffusivity_edges, wind_edges, values_near, errors_near, flags_near, flags_far = scratch[7 * n : 7 * n + 6]
    where_near, where_far, blocks, once, factors, averaged, *sems = scratch[7 * n + 6 :]
    up_send, down_send, low_recv, high_recv, relay_send, relay_recv = sems[:6]
    spread_send, spread_recv, hop_send, hop_recv, send, recv, table = sems[6:]
    mem, lat = lax.axis_index("mem"), lax.axis_index("lat")
    z, c, h, s, w = place()
    mine = w * 2 + c
    group = member(z, w, c)
    patch = group * 2 + c

    def peer(i):
        dx, dy, dc = PEERS[i - 1]
        k = ((w // 2 + dx) % 4) * 4 + ((w + dy) % 2) * 2 + (c + dc) % 2
        return k, device(z, k % 2, h, s, k // 2)

    hops = lane(w, z, c) != z
    hop_to, hop_from = device(lane(w, z, c), c, h, s, w), device(group, c, h, s, w)
    up_far, down_far = (lat == 15) & (mem != 15), (lat == 16) & (mem != 0)
    up_near, down_near = (lat < 31) & jnp.logical_not(up_far), (lat > 0) & jnp.logical_not(down_far)
    relays_up, relays_down = (lat == mem) & (lat != 15), (lat == mem + 16) & (lat != 16)
    relays = relays_up | relays_down
    low_from = (mem, jnp.where((lat == 16) & (mem != 15), mem, jnp.maximum(lat - 1, 0)))
    high_from = (mem, jnp.where((lat == 15) & (mem != 0), mem + 16, jnp.minimum(lat + 1, 31)))
    relay_from = (mem, jnp.where(relays_up, 15, 16))
    enter(
        lambda i: peer(i)[1],
        ((hops, hop_from), (lat > 0, low_from), (lat < 31, high_from), (relays, relay_from)),
        (hops, lat < 31, lat > 0, relays),
    )

    def remote(source, target, sends, recvs, i, to):
        return pltpu.make_async_remote_copy(
            source, target, sends.at[i], recvs.at[i], device_id=to, device_id_type=MESH
        )

    class Edge:
        def __init__(self, i):
            if i < 2:
                ref, ends = ((diffusivity, diffusivity_edges), (north_wind, wind_edges))[i]
                first, last = ref.at[pl.ds(0, 1)], ref.at[pl.ds(7, 1)]
                bottom, top, held = ends.at[0], ends.at[1], ends.at[2]
            else:
                part = rows(OUT, i - 2)
                first, last = field.at[pl.ds(0, 8), part], field.at[pl.ds(24, 8), part]
                bottom, top, held = low[i - 2], high[i - 2], relay[i - 2]
            above, below = (mem, jnp.minimum(lat + 1, 31)), (mem, jnp.maximum(lat - 1, 0))
            self.bottom, self.top = bottom, top
            self.ups = (
                (up_near, remote(last, bottom, up_send, low_recv, i, above)),
                (up_far, remote(last, held, up_send, relay_recv, i, (mem, mem))),
            )
            self.downs = (
                (down_near, remote(first, top, down_send, high_recv, i, below)),
                (down_far, remote(first, held, down_send, relay_recv, i, (mem, mem + 16))),
            )
            self.passes = (
                (relays_up, remote(held, bottom, relay_send, low_recv, i, (mem, 16))),
                (relays_down, remote(held, top, relay_send, high_recv, i, (mem, 15))),
            )

        def start(self, far):
            for there, copy in (self.ups[far], self.downs[far]):
                pl.when(there)(copy.start)

        def fill(self):
            @pl.when(lat == 0)
            def _():
                self.bottom[...] = jnp.zeros(self.bottom.shape, jnp.float32)

            @pl.when(lat == 31)
            def _():
                self.top[...] = jnp.zeros(self.top.shape, jnp.float32)

        def forward(self):
            for (there, copy), (_, arriving) in zip(self.passes, (self.ups[1], self.downs[1])):

                @pl.when(there)
                def _():
                    arriving.wait_recv()
                    copy.start()

        def wait(self):
            pl.when(lat > 0)(self.ups[0][1].wait_recv)
            pl.when(lat < 31)(self.downs[0][1].wait_recv)

        def end(self):
            for there, copy in self.ups + self.downs + self.passes:
                pl.when(there)(copy.wait_send)

    spread_to = device(z, c, h, s, lane(w, z, c))
    spreads = lane(w, z, c) != w
    parts = list(zip(cast, near, far)) + [
        (flags, flags_near, flags_far),
        (where, where_near, where_far),
        (values, values_near, values_out),
        (errors, errors_near, errors_out),
    ]
    spread = [Move(a, b, spread_send.at[i], spread_recv.at[i], spread_to, spreads) for i, (a, b, _) in enumerate(parts)]
    hop = [Move(b, d, hop_send.at[i], hop_recv.at[i], hop_to, hops) for i, (_, b, d) in enumerate(parts)]

    def piece(i, off):
        k, there = peer(off)
        wanted = member(z, k // 2, k % 2) * 2 + k % 2
        return pltpu.make_async_remote_copy(
            stage[i].at[wanted],
            out.at[mine, rows(OUT, i)],
            send.at[i, off],
            recv.at[i, off],
            device_id=there,
            device_id_type=MESH,
        )

    def own(i):
        return pltpu.make_async_copy(stage[i].at[patch], out.at[mine, rows(OUT, i)], recv.at[i, 0])

    def ends(i):
        column = lax.broadcasted_iota(jnp.int32, (OUT[i], 128), 1)
        return column == 0, column == 127

    def tile(k):
        return [factors[k, q : q + 1] for q in range(8)]

    def forecast(i):
        size, part = OUT[i], rows(OUT, i)
        first_lane, last_lane = ends(i)

        def before(k):
            if isinstance(k, int) and k < 2:
                return [low[i][4 * k + q] for q in range(4)]
            if isinstance(k, int) and k > 9:
                return [high[i][4 * k - 40 + q] for q in range(4)]
            return [field[4 * k - 8 + q, part] for q in range(4)]

        def middle(k):
            return [once[4 * k + q, :size] for q in range(4)]

        def first(r):
            new = advance(before(r + 1), before(r), before(r + 2), tile(r), first_lane, last_lane)
            for q in range(4):
                once[4 * r + q, :size] = new[q]

        for r in (0, 1, 8, 9):
            first(r)
        pl.loop(2, 8)(first)

        @pl.loop(0, 8)
        def _(r):
            new = advance(middle(r + 1), middle(r), middle(r + 2), tile(r + 1), first_lane, last_lane)
            for q in range(4):
                cast[i][4 * r + q] = new[q]

    def observe(i):
        tiles, put = far[i], stage[i]
        first_lane, _ = ends(i)

        @pl.loop(0, 8)
        def _(half):
            for p in range(2):
                for t in range(2):
                    put[2 * half + p, :, t * 128 : (t + 1) * 128] = tiles[4 * half + 2 * p + t]
                for j in range(4):
                    at = half * 8 + p * 4 + j
                    direct = tiles[blocks[0, at]]
                    beside = jnp.where(first_lane, tiles[blocks[1, at]], direct)
                    east = pltpu.roll(beside, 127, 1)
                    flag = averaged[half, p * 4 + j : p * 4 + j + 1]
                    seen = jnp.where(flag == 1, 0.5 * (direct + east), direct)
                    put[2 * half + p, :, 256 + j * 128 : 384 + j * 128] = seen

        for off in range(1, 16):
            piece(i, off).start()

        own(i).start()

    edges = [Edge(i) for i in range(n + 2)]
    for edge in edges:
        edge.start(1)
    for edge in edges:
        edge.start(0)
    for edge in edges:
        edge.fill()
    for edge in edges:
        edge.forward()
    for move in spread[n:]:
        move.start()
    for k, ref in enumerate((diffusivity, north_wind)):
        for q in range(4):
            for r in range(8):
                factors[r + 1, 4 * k + q : 4 * k + q + 1] = ref[r : r + 1, q * 128 : (q + 1) * 128]
    for k, ref in enumerate((diffusivity_edges, wind_edges)):
        edges[k].wait()
        for q in range(4):
            for at, r in ((0, 0), (1, 9)):
                factors[r, 4 * k + q : 4 * k + q + 1] = ref[at, :, q * 128 : (q + 1) * 128]
    for i in range(n):
        edges[i + 2].wait()
        forecast(i)
        spread[i].start()
        if i == 1:
            for move, after in zip(spread[n:] + spread[:1], hop[n:] + hop[:1]):
                move.wait_recv()
                after.start()
    for i in range(n):
        if i + 1 < n:
            spread[i + 1].wait_recv()
            hop[i + 1].start()
        if i == 0:
            for move in hop[n:]:
                move.wait_recv()
            for p in range(16):
                for j in range(4):
                    at = p % 2 * 4 + j
                    averaged[p // 2, at : at + 1] = flags_far[p : p + 1, j * 128 : (j + 1) * 128]
            read = pltpu.make_async_copy(where_far, blocks, table)
            read.start()
            read.wait()
        hop[i].wait_recv()
        observe(i)
    for edge in edges:
        edge.end()
    for move in spread + hop:
        move.wait_send()
    for i in range(n):

        for off in range(1, 16):
            piece(i, off).wait()

        own(i).wait()


def gather(field, diffusivity, north_wind, flags, values, errors, where):
    def buffer(*shape, dtype=jnp.float32):
        return pltpu.VMEM(shape, dtype)

    n = len(OUT)
    dma, table = pltpu.SemaphoreType.DMA, buffer(8, 128, dtype=jnp.int32)
    vmem = pl.BlockSpec(memory_space=pltpu.VMEM)
    row = jax.ShapeDtypeStruct((1, 512), jnp.float32)
    return pl.pallas_call(
        gather_kernel,
        out_shape=(jax.ShapeDtypeStruct((16, MEMBERS, 768), jnp.float32), row, row),
        in_specs=[vmem] * 7,
        out_specs=(vmem,) * 3,
        scratch_shapes=[buffer(8, size, 128) for size in OUT * 3]
        + [buffer(32, size, 128) for size in OUT * 3]
        + [buffer(16, size, 768) for size in OUT]
        + [buffer(3, 1, 512)] * 2
        + [buffer(1, 512)] * 2
        + [buffer(16, 512, dtype=jnp.int32)] * 2
        + [table, table, pltpu.SMEM((8, 128), jnp.int32), buffer(40, max(OUT), 128)]
        + [buffer(10, 8, 128), buffer(8, 8, 128, dtype=jnp.int32)]
        + [dma((n + 2,))] * 6
        + [dma((n + 4,))] * 4
        + [dma((n, 16))] * 2
        + [dma],
        compiler_params=pltpu.CompilerParams(
            collective_id=0, has_side_effects=True, vmem_limit_bytes=40 * 2**20
        ),
        name="gather",
    )(field, diffusivity, north_wind, flags, values, errors, where)


def scatter_kernel(cells, out, *scratch):
    held = scratch[:len(BACK)]
    home_send, home_recv, send, recv = scratch[len(BACK):]
    z, c, h, s, w = place()
    mine = w * 2 + c
    group = member(z, w, c)
    patch = group * 2 + c

    def peer(i):
        dx, dy, dc = PEERS[i - 1]
        k = ((w // 2 + dx) % 4) * 4 + ((w + dy) % 2) * 2 + (c + dc) % 2
        return k, device(z, k % 2, h, s, k // 2)

    home, guest = device(group, c, h, s, z), device(w, c, h, s, lane(w, z, c))
    away = jnp.logical_or(w != z, group != z)
    enter(lambda i: peer(i)[1], ((away, guest),), (away,))

    def piece(i, off):
        k, where = peer(off)
        return pltpu.make_async_remote_copy(
            cells.at[k, rows(BACK, i)],
            held[i].at[patch],
            send.at[i, off],
            recv.at[i, off],
            device_id=where,
            device_id_type=MESH,
        )

    def own(i):
        return pltpu.make_async_copy(cells.at[mine, rows(BACK, i)], held[i].at[patch], recv.at[i, 0])

    def start(i):
        for off in range(1, 16):
            piece(i, off).start()

        own(i).start()

    back = [
        Move(held[i], out.at[:, rows(BACK, i)], home_send.at[i], home_recv.at[i], home, away)
        for i in range(len(BACK))
    ]
    start(0)
    for i in range(len(BACK)):

        for off in range(1, 16):
            piece(i, off).wait_recv()

        own(i).wait()
        back[i].start()
        if i + 1 < len(BACK):
            start(i + 1)
    for i in range(len(BACK)):
        back[i].wait_recv()
        back[i].wait_send()

        for off in range(1, 16):
            piece(i, off).wait_send()


def scatter(cells):
    dma = pltpu.SemaphoreType.DMA
    vmem = pl.BlockSpec(memory_space=pltpu.VMEM)
    return pl.pallas_call(
        scatter_kernel,
        out_shape=jax.ShapeDtypeStruct((16, MEMBERS, 256), jnp.float32),
        in_specs=[vmem],
        out_specs=vmem,
        scratch_shapes=[pltpu.VMEM((16, size, 256), jnp.float32) for size in BACK]
        + [dma((len(BACK),))] * 2
        + [dma((len(BACK), 16))] * 2,
        compiler_params=pltpu.CompilerParams(
            collective_id=1, has_side_effects=True, vmem_limit_bytes=40 * 2**20
        ),
        name="scatter",
    )(cells)


def dot(left, right):
    return jnp.dot(left, right, precision=PREC, preferred_element_type=jnp.float32)


def analyse(states, values, errors):
    count = states.shape[0]
    mean = jnp.mean(states, axis=0)
    offset = states - mean
    seen_offset = offset[:, 256:]
    products = lax.dot_general(
        offset, seen_offset, (((0,), (0,)), ((), ())), precision=PREC, preferred_element_type=jnp.float32
    ) / (count - 1.0)
    covariance = products[256:] + jnp.diag(errors)
    scale = lax.rsqrt(jnp.sum(jnp.abs(covariance), axis=1))
    power = jnp.eye(512, dtype=jnp.float32) - covariance * scale[:, None] * scale[None, :]
    gain = products[:256] * scale[None, :]
    for step in range(4):
        gain = gain + dot(gain, power)
        if step < 3:
            power = dot(power, power)
    gain = gain * scale[None, :]
    weights = (values - mean[256:])[None, :] - 0.5 * seen_offset
    update = lax.dot_general(
        weights, gain, (((1,), (1,)), ((), ())), precision=PREC, preferred_element_type=jnp.float32
    )
    return states[:, :256] + update


def body(ensemble, diffusivity, north_wind, observed_blocks, eastern_average_flags, observed_values, observed_error):
    blocks = observed_blocks[0].reshape(1, 64)
    nexts = blocks - blocks % 4 + (blocks + 1) % 4
    where = jnp.pad(jnp.concatenate([blocks, nexts]), ((0, 6), (0, 64)))
    field = ensemble.reshape(MEMBERS, 8, 4, 128).transpose(1, 2, 0, 3).reshape(32, MEMBERS, 128)
    states, values, errors = gather(
        field, diffusivity, north_wind, eastern_average_flags[0], observed_values[0], observed_error[0], where
    )
    states, values, errors = states.reshape(16 * MEMBERS, 768), values[0], errors[0]
    cells = analyse(states, values, errors).reshape(16, MEMBERS, 256)
    out = scatter(cells)
    return out.reshape(8, 2, MEMBERS, 256).transpose(2, 0, 1, 3).reshape(MEMBERS, 8, 512)


def solution(mesh):
    return jax.shard_map(
        body,
        mesh=mesh,
        in_specs=(
            P("mem", "lat", None),
            P("lat", None),
            P("lat", None),
            P("lat", None, None),
            P("lat", None, None),
            P("lat", "mem", None),
            P("lat", "mem", None),
        ),
        out_specs=P("mem", "lat", None),
        check_vma=False,
    )
```

```python
import jax
import jax.numpy as jnp
from jax import lax
from jax.experimental import pallas as pl
from jax.experimental.pallas import tpu as pltpu
from jax.sharding import PartitionSpec as P

MESH = pl.DeviceIdType.MESH
ADVECTION = 0.1
MEMBERS = 64
OUT = (16, 16, 16, 16)
BACK = (16, 16, 16, 16)
PREC = lax.Precision.HIGH

PEERS = (
    (0, 1, 0), (1, 0, 0), (3, 0, 0), (2, 1, 0), (1, 1, 0), (3, 1, 0), (2, 0, 0), (0, 1, 1),
    (1, 0, 1), (3, 0, 1), (2, 1, 1), (0, 0, 1), (1, 1, 1), (3, 1, 1), (2, 0, 1),
)

SPIN, SIDE = (7, 3, 5), 5


def both(*values):
    return sum(sum(v // 2**i % 2 for v in values) % 2 * 2**i for i in range(3))


def mix(rows, v):
    return sum(sum(v // 2**j % 2 for j in range(3) if rows[i] // 2**j % 2) % 2 * 2**i for i in range(3))


UNSPIN = next(
    rows
    for rows in ((i, j, k) for i in range(8) for j in range(8) for k in range(8))
    if all(mix(rows, mix(SPIN, v)) == v for v in range(8))
)


def lane(w, z, c):
    return both(w, mix(SPIN, z), SIDE * c)


def member(z, w, c):
    return mix(UNSPIN, both(z, w, SIDE * c))


def device(z, c, h, s, w):
    return (z * 2 + c, h * 16 + (w // 2) * 4 + s * 2 + w % 2)


def place():
    m, l = lax.axis_index("mem"), lax.axis_index("lat")
    return m // 2, m % 2, l // 16, (l % 4) // 2, ((l // 4) % 4) * 2 + l % 2


def enter(peers, sources, targets):
    barrier = pltpu.get_barrier_semaphore()

    for i in range(1, 16):
        pl.semaphore_signal(barrier, inc=1, device_id=peers(i), device_id_type=MESH)

    for there, source in sources:

        @pl.when(there)
        def _():
            pl.semaphore_signal(barrier, inc=1, device_id=source, device_id_type=MESH)

    count = 15
    for there in targets:
        count = count + jnp.where(there, 1, 0)
    pl.semaphore_wait(barrier, count)


def rows(sizes, i):
    return pl.ds(sum(sizes[:i]), sizes[i])


class Move:
    def __init__(self, source, target, send, recv, where, away):
        self.away, self.home = away, jnp.logical_not(away)
        self.remote = pltpu.make_async_remote_copy(
            source, target, send, recv, device_id=where, device_id_type=MESH
        )
        self.local = pltpu.make_async_copy(source, target, recv)

    def start(self):
        pl.when(self.away)(self.remote.start)
        pl.when(self.home)(self.local.start)

    def wait_recv(self):
        pl.when(self.away)(self.remote.wait_recv)
        pl.when(self.home)(self.local.wait)

    def wait_send(self):
        pl.when(self.away)(self.remote.wait_send)


def advance(centre, north, south, terms, first_lane, last_lane):
    out = []
    for q in range(4):
        mid = centre[q]
        east = pltpu.roll(jnp.where(first_lane, centre[(q + 1) % 4], mid), 127, 1)
        west = pltpu.roll(jnp.where(last_lane, centre[(q + 3) % 4], mid), 1, 1)
        out.append(
            mid
            - ADVECTION * mid * (east - west)
            - terms[4 + q] * (south[q] - north[q])
            + terms[q] * (east + west + north[q] + south[q] - 4.0 * mid)
        )
    return out


def gather_kernel(field, diffusivity, north_wind, flags, values, errors, where, out, *rest):
    n = len(OUT)
    values_out, errors_out, *scratch = rest
    low, high, relay, cast, near, far, stage = (scratch[n * k : n * (k + 1)] for k in range(7))
    diffusivity_edges, wind_edges, values_near, errors_near, flags_near, flags_far = scratch[7 * n : 7 * n + 6]
    where_near, where_far, blocks, once, factors, averaged, *sems = scratch[7 * n + 6 :]
    up_send, down_send, low_recv, high_recv, relay_send, relay_recv = sems[:6]
    spread_send, spread_recv, hop_send, hop_recv, send, recv, table = sems[6:]
    mem, lat = lax.axis_index("mem"), lax.axis_index("lat")
    z, c, h, s, w = place()
    mine = w * 2 + c
    group = member(z, w, c)
    patch = group * 2 + c

    def peer(i):
        dx, dy, dc = PEERS[i - 1]
        k = ((w // 2 + dx) % 4) * 4 + ((w + dy) % 2) * 2 + (c + dc) % 2
        return k, device(z, k % 2, h, s, k // 2)

    hops = lane(w, z, c) != z
    hop_to, hop_from = device(lane(w, z, c), c, h, s, w), device(group, c, h, s, w)
    up_far, down_far = (lat == 15) & (mem != 15), (lat == 16) & (mem != 0)
    up_near, down_near = (lat < 31) & jnp.logical_not(up_far), (lat > 0) & jnp.logical_not(down_far)
    relays_up, relays_down = (lat == mem) & (lat != 15), (lat == mem + 16) & (lat != 16)
    relays = relays_up | relays_down
    low_from = (mem, jnp.where((lat == 16) & (mem != 15), mem, jnp.maximum(lat - 1, 0)))
    high_from = (mem, jnp.where((lat == 15) & (mem != 0), mem + 16, jnp.minimum(lat + 1, 31)))
    relay_from = (mem, jnp.where(relays_up, 15, 16))
    enter(
        lambda i: peer(i)[1],
        ((hops, hop_from), (lat > 0, low_from), (lat < 31, high_from), (relays, relay_from)),
        (hops, lat < 31, lat > 0, relays),
    )

    def remote(source, target, sends, recvs, i, to):
        return pltpu.make_async_remote_copy(
            source, target, sends.at[i], recvs.at[i], device_id=to, device_id_type=MESH
        )

    class Edge:
        def __init__(self, i):
            if i < 2:
                ref, ends = ((diffusivity, diffusivity_edges), (north_wind, wind_edges))[i]
                first, last = ref.at[pl.ds(0, 1)], ref.at[pl.ds(7, 1)]
                bottom, top, held = ends.at[0], ends.at[1], ends.at[2]
            else:
                part = rows(OUT, i - 2)
                first, last = field.at[pl.ds(0, 8), part], field.at[pl.ds(24, 8), part]
                bottom, top, held = low[i - 2], high[i - 2], relay[i - 2]
            above, below = (mem, jnp.minimum(lat + 1, 31)), (mem, jnp.maximum(lat - 1, 0))
            self.bottom, self.top = bottom, top
            self.ups = (
                (up_near, remote(last, bottom, up_send, low_recv, i, above)),
                (up_far, remote(last, held, up_send, relay_recv, i, (mem, mem))),
            )
            self.downs = (
                (down_near, remote(first, top, down_send, high_recv, i, below)),
                (down_far, remote(first, held, down_send, relay_recv, i, (mem, mem + 16))),
            )
            self.passes = (
                (relays_up, remote(held, bottom, relay_send, low_recv, i, (mem, 16))),
                (relays_down, remote(held, top, relay_send, high_recv, i, (mem, 15))),
            )

        def start(self, far):
            for there, copy in (self.ups[far], self.downs[far]):
                pl.when(there)(copy.start)

        def fill(self):
            @pl.when(lat == 0)
            def _():
                self.bottom[...] = jnp.zeros(self.bottom.shape, jnp.float32)

            @pl.when(lat == 31)
            def _():
                self.top[...] = jnp.zeros(self.top.shape, jnp.float32)

        def forward(self):
            for (there, copy), (_, arriving) in zip(self.passes, (self.ups[1], self.downs[1])):

                @pl.when(there)
                def _():
                    arriving.wait_recv()
                    copy.start()

        def wait(self):
            pl.when(lat > 0)(self.ups[0][1].wait_recv)
            pl.when(lat < 31)(self.downs[0][1].wait_recv)

        def end(self):
            for there, copy in self.ups + self.downs + self.passes:
                pl.when(there)(copy.wait_send)

    spread_to = device(z, c, h, s, lane(w, z, c))
    spreads = lane(w, z, c) != w
    parts = list(zip(cast, near, far)) + [
        (flags, flags_near, flags_far),
        (where, where_near, where_far),
        (values, values_near, values_out),
        (errors, errors_near, errors_out),
    ]
    spread = [Move(a, b, spread_send.at[i], spread_recv.at[i], spread_to, spreads) for i, (a, b, _) in enumerate(parts)]
    hop = [Move(b, d, hop_send.at[i], hop_recv.at[i], hop_to, hops) for i, (_, b, d) in enumerate(parts)]

    def piece(i, off):
        k, there = peer(off)
        wanted = member(z, k // 2, k % 2) * 2 + k % 2
        return pltpu.make_async_remote_copy(
            stage[i].at[wanted],
            out.at[mine, rows(OUT, i)],
            send.at[i, off],
            recv.at[i, off],
            device_id=there,
            device_id_type=MESH,
        )

    def own(i):
        return pltpu.make_async_copy(stage[i].at[patch], out.at[mine, rows(OUT, i)], recv.at[i, 0])

    def ends(i):
        column = lax.broadcasted_iota(jnp.int32, (OUT[i], 128), 1)
        return column == 0, column == 127

    def tile(k):
        return [factors[k, q : q + 1] for q in range(8)]

    def forecast(i):
        size, part = OUT[i], rows(OUT, i)
        first_lane, last_lane = ends(i)

        def before(k):
            if isinstance(k, int) and k < 2:
                return [low[i][4 * k + q] for q in range(4)]
            if isinstance(k, int) and k > 9:
                return [high[i][4 * k - 40 + q] for q in range(4)]
            return [field[4 * k - 8 + q, part] for q in range(4)]

        def middle(k):
            return [once[4 * k + q, :size] for q in range(4)]

        def first(r):
            new = advance(before(r + 1), before(r), before(r + 2), tile(r), first_lane, last_lane)
            for q in range(4):
                once[4 * r + q, :size] = new[q]

        for r in (0, 1, 8, 9):
            first(r)
        pl.loop(2, 8)(first)

        @pl.loop(0, 8)
        def _(r):
            new = advance(middle(r + 1), middle(r), middle(r + 2), tile(r + 1), first_lane, last_lane)
            for q in range(4):
                cast[i][4 * r + q] = new[q]

    def observe(i):
        tiles, put = far[i], stage[i]
        first_lane, _ = ends(i)

        @pl.loop(0, 8)
        def _(half):
            for p in range(2):
                for t in range(2):
                    put[2 * half + p, :, t * 128 : (t + 1) * 128] = tiles[4 * half + 2 * p + t]
                for j in range(4):
                    at = half * 8 + p * 4 + j
                    direct = tiles[blocks[0, at]]
                    beside = jnp.where(first_lane, tiles[blocks[1, at]], direct)
                    east = pltpu.roll(beside, 127, 1)
                    flag = averaged[half, p * 4 + j : p * 4 + j + 1]
                    seen = jnp.where(flag == 1, 0.5 * (direct + east), direct)
                    put[2 * half + p, :, 256 + j * 128 : 384 + j * 128] = seen

        for off in range(1, 16):
            piece(i, off).start()

        own(i).start()

    edges = [Edge(i) for i in range(n + 2)]
    for edge in edges:
        edge.start(1)
    for edge in edges[:3]:
        edge.start(0)
    for edge in edges:
        edge.fill()
    for edge in edges:
        edge.forward()
    for edge in edges[3:]:
        edge.start(0)
    for move in spread[n:]:
        move.start()
    for k, ref in enumerate((diffusivity, north_wind)):
        for q in range(4):
            for r in range(8):
                factors[r + 1, 4 * k + q : 4 * k + q + 1] = ref[r : r + 1, q * 128 : (q + 1) * 128]
    for k, ref in enumerate((diffusivity_edges, wind_edges)):
        edges[k].wait()
        for q in range(4):
            for at, r in ((0, 0), (1, 9)):
                factors[r, 4 * k + q : 4 * k + q + 1] = ref[at, :, q * 128 : (q + 1) * 128]
    for i in range(n):
        edges[i + 2].wait()
        forecast(i)
        spread[i].start()
        if i == 1:
            for move, after in zip(spread[n:] + spread[:1], hop[n:] + hop[:1]):
                move.wait_recv()
                after.start()
    for i in range(n):
        if i + 1 < n:
            spread[i + 1].wait_recv()
            hop[i + 1].start()
        if i == 0:
            for move in hop[n:]:
                move.wait_recv()
            for p in range(16):
                for j in range(4):
                    at = p % 2 * 4 + j
                    averaged[p // 2, at : at + 1] = flags_far[p : p + 1, j * 128 : (j + 1) * 128]
            read = pltpu.make_async_copy(where_far, blocks, table)
            read.start()
            read.wait()
        hop[i].wait_recv()
        observe(i)
    for edge in edges:
        edge.end()
    for move in spread + hop:
        move.wait_send()
    for i in range(n):

        for off in range(1, 16):
            piece(i, off).wait()

        own(i).wait()


def gather(field, diffusivity, north_wind, flags, values, errors, where):
    def buffer(*shape, dtype=jnp.float32):
        return pltpu.VMEM(shape, dtype)

    n = len(OUT)
    dma, table = pltpu.SemaphoreType.DMA, buffer(8, 128, dtype=jnp.int32)
    vmem = pl.BlockSpec(memory_space=pltpu.VMEM)
    row = jax.ShapeDtypeStruct((1, 512), jnp.float32)
    return pl.pallas_call(
        gather_kernel,
        out_shape=(jax.ShapeDtypeStruct((16, MEMBERS, 768), jnp.float32), row, row),
        in_specs=[vmem] * 7,
        out_specs=(vmem,) * 3,
        scratch_shapes=[buffer(8, size, 128) for size in OUT * 3]
        + [buffer(32, size, 128) for size in OUT * 3]
        + [buffer(16, size, 768) for size in OUT]
        + [buffer(3, 1, 512)] * 2
        + [buffer(1, 512)] * 2
        + [buffer(16, 512, dtype=jnp.int32)] * 2
        + [table, table, pltpu.SMEM((8, 128), jnp.int32), buffer(40, max(OUT), 128)]
        + [buffer(10, 8, 128), buffer(8, 8, 128, dtype=jnp.int32)]
        + [dma((n + 2,))] * 6
        + [dma((n + 4,))] * 4
        + [dma((n, 16))] * 2
        + [dma],
        compiler_params=pltpu.CompilerParams(
            collective_id=0, has_side_effects=True, vmem_limit_bytes=40 * 2**20
        ),
        name="gather",
    )(field, diffusivity, north_wind, flags, values, errors, where)


def scatter_kernel(cells, out, *scratch):
    held = scratch[:len(BACK)]
    home_send, home_recv, send, recv = scratch[len(BACK):]
    z, c, h, s, w = place()
    mine = w * 2 + c
    group = member(z, w, c)
    patch = group * 2 + c

    def peer(i):
        dx, dy, dc = PEERS[i - 1]
        k = ((w // 2 + dx) % 4) * 4 + ((w + dy) % 2) * 2 + (c + dc) % 2
        return k, device(z, k % 2, h, s, k // 2)

    home, guest = device(group, c, h, s, z), device(w, c, h, s, lane(w, z, c))
    away = jnp.logical_or(w != z, group != z)
    enter(lambda i: peer(i)[1], ((away, guest),), (away,))

    def piece(i, off):
        k, where = peer(off)
        return pltpu.make_async_remote_copy(
            cells.at[k, rows(BACK, i)],
            held[i].at[patch],
            send.at[i, off],
            recv.at[i, off],
            device_id=where,
            device_id_type=MESH,
        )

    def own(i):
        return pltpu.make_async_copy(cells.at[mine, rows(BACK, i)], held[i].at[patch], recv.at[i, 0])

    def start(i):
        for off in range(1, 16):
            piece(i, off).start()

        own(i).start()

    back = [
        Move(held[i], out.at[:, rows(BACK, i)], home_send.at[i], home_recv.at[i], home, away)
        for i in range(len(BACK))
    ]
    start(0)
    for i in range(len(BACK)):

        for off in range(1, 16):
            piece(i, off).wait_recv()

        own(i).wait()
        back[i].start()
        if i + 1 < len(BACK):
            start(i + 1)
    for i in range(len(BACK)):
        back[i].wait_recv()
        back[i].wait_send()

        for off in range(1, 16):
            piece(i, off).wait_send()


def scatter(cells):
    dma = pltpu.SemaphoreType.DMA
    vmem = pl.BlockSpec(memory_space=pltpu.VMEM)
    return pl.pallas_call(
        scatter_kernel,
        out_shape=jax.ShapeDtypeStruct((16, MEMBERS, 256), jnp.float32),
        in_specs=[vmem],
        out_specs=vmem,
        scratch_shapes=[pltpu.VMEM((16, size, 256), jnp.float32) for size in BACK]
        + [dma((len(BACK),))] * 2
        + [dma((len(BACK), 16))] * 2,
        compiler_params=pltpu.CompilerParams(
            collective_id=1, has_side_effects=True, vmem_limit_bytes=40 * 2**20
        ),
        name="scatter",
    )(cells)


def dot(left, right):
    return jnp.dot(left, right, precision=PREC, preferred_element_type=jnp.float32)


def analyse(states, values, errors):
    count = states.shape[0]
    mean = jnp.mean(states, axis=0)
    offset = states - mean
    seen_offset = offset[:, 256:]
    products = lax.dot_general(
        offset, seen_offset, (((0,), (0,)), ((), ())), precision=PREC, preferred_element_type=jnp.float32
    ) / (count - 1.0)
    covariance = products[256:] + jnp.diag(errors)
    scale = lax.rsqrt(jnp.sum(jnp.abs(covariance), axis=1))
    power = jnp.eye(512, dtype=jnp.float32) - covariance * scale[:, None] * scale[None, :]
    gain = products[:256] * scale[None, :]
    for _ in range(3):
        both_products = dot(jnp.concatenate([gain, power]), power)
        gain, power = gain + both_products[:256], both_products[256:]
    gain = (gain + dot(gain, power)) * scale[None, :]
    weights = (values - mean[256:])[None, :] - 0.5 * seen_offset
    update = lax.dot_general(
        weights, gain, (((1,), (1,)), ((), ())), precision=PREC, preferred_element_type=jnp.float32
    )
    return states[:, :256] + update


def body(ensemble, diffusivity, north_wind, observed_blocks, eastern_average_flags, observed_values, observed_error):
    blocks = observed_blocks[0].reshape(1, 64)
    nexts = blocks - blocks % 4 + (blocks + 1) % 4
    where = jnp.pad(jnp.concatenate([blocks, nexts]), ((0, 6), (0, 64)))
    field = ensemble.reshape(MEMBERS, 8, 4, 128).transpose(1, 2, 0, 3).reshape(32, MEMBERS, 128)
    states, values, errors = gather(
        field, diffusivity, north_wind, eastern_average_flags[0], observed_values[0], observed_error[0], where
    )
    states, values, errors = states.reshape(16 * MEMBERS, 768), values[0], errors[0]
    cells = analyse(states, values, errors).reshape(16, MEMBERS, 256)
    out = scatter(cells)
    return out.reshape(8, 2, MEMBERS, 256).transpose(2, 0, 1, 3).reshape(MEMBERS, 8, 512)


def solution(mesh):
    return jax.shard_map(
        body,
        mesh=mesh,
        in_specs=(
            P("mem", "lat", None),
            P("lat", None),
            P("lat", None),
            P("lat", None, None),
            P("lat", None, None),
            P("lat", "mem", None),
            P("lat", "mem", None),
        ),
        out_specs=P("mem", "lat", None),
        check_vma=False,
    )
```

```python
import jax
import jax.numpy as jnp
from jax import lax
from jax.experimental import pallas as pl
from jax.experimental.pallas import tpu as pltpu
from jax.sharding import PartitionSpec as P

MESH = pl.DeviceIdType.MESH
ADVECTION = 0.1
MEMBERS = 64
OUT = (8, 16, 16, 16, 8)
BACK = (16, 16, 16, 16)
PREC = lax.Precision.HIGH

PEERS = (
    (0, 1, 0), (1, 0, 0), (3, 0, 0), (2, 1, 0), (1, 1, 0), (3, 1, 0), (2, 0, 0), (0, 1, 1),
    (1, 0, 1), (3, 0, 1), (2, 1, 1), (0, 0, 1), (1, 1, 1), (3, 1, 1), (2, 0, 1),
)

SPIN, SIDE = (7, 3, 5), 5


def both(*values):
    return sum(sum(v // 2**i % 2 for v in values) % 2 * 2**i for i in range(3))


def mix(rows, v):
    return sum(sum(v // 2**j % 2 for j in range(3) if rows[i] // 2**j % 2) % 2 * 2**i for i in range(3))


UNSPIN = next(
    rows
    for rows in ((i, j, k) for i in range(8) for j in range(8) for k in range(8))
    if all(mix(rows, mix(SPIN, v)) == v for v in range(8))
)


def lane(w, z, c):
    return both(w, mix(SPIN, z), SIDE * c)


def member(z, w, c):
    return mix(UNSPIN, both(z, w, SIDE * c))


def device(z, c, h, s, w):
    return (z * 2 + c, h * 16 + (w // 2) * 4 + s * 2 + w % 2)


def place():
    m, l = lax.axis_index("mem"), lax.axis_index("lat")
    return m // 2, m % 2, l // 16, (l % 4) // 2, ((l // 4) % 4) * 2 + l % 2


def enter(peers, sources, targets):
    barrier = pltpu.get_barrier_semaphore()

    for i in range(1, 16):
        pl.semaphore_signal(barrier, inc=1, device_id=peers(i), device_id_type=MESH)

    for there, source in sources:

        @pl.when(there)
        def _():
            pl.semaphore_signal(barrier, inc=1, device_id=source, device_id_type=MESH)

    count = 15
    for there in targets:
        count = count + jnp.where(there, 1, 0)
    pl.semaphore_wait(barrier, count)


def rows(sizes, i):
    return pl.ds(sum(sizes[:i]), sizes[i])


class Move:
    def __init__(self, source, target, send, recv, where, away):
        self.away, self.home = away, jnp.logical_not(away)
        self.remote = pltpu.make_async_remote_copy(
            source, target, send, recv, device_id=where, device_id_type=MESH
        )
        self.local = pltpu.make_async_copy(source, target, recv)

    def start(self):
        pl.when(self.away)(self.remote.start)
        pl.when(self.home)(self.local.start)

    def wait_recv(self):
        pl.when(self.away)(self.remote.wait_recv)
        pl.when(self.home)(self.local.wait)

    def wait_send(self):
        pl.when(self.away)(self.remote.wait_send)


def advance(centre, north, south, terms, first_lane, last_lane):
    out = []
    for q in range(4):
        mid = centre[q]
        east = pltpu.roll(jnp.where(first_lane, centre[(q + 1) % 4], mid), 127, 1)
        west = pltpu.roll(jnp.where(last_lane, centre[(q + 3) % 4], mid), 1, 1)
        out.append(
            mid
            - ADVECTION * mid * (east - west)
            - terms[4 + q] * (south[q] - north[q])
            + terms[q] * (east + west + north[q] + south[q] - 4.0 * mid)
        )
    return out


def gather_kernel(field, diffusivity, north_wind, flags, values, errors, where, out, *rest):
    n = len(OUT)
    values_out, errors_out, *scratch = rest
    low, high, relay, cast, near, far, stage = (scratch[n * k : n * (k + 1)] for k in range(7))
    diffusivity_edges, wind_edges, values_near, errors_near, flags_near, flags_far = scratch[7 * n : 7 * n + 6]
    where_near, where_far, blocks, once, factors, averaged, *sems = scratch[7 * n + 6 :]
    up_send, down_send, low_recv, high_recv, relay_send, relay_recv = sems[:6]
    spread_send, spread_recv, hop_send, hop_recv, send, recv, table = sems[6:]
    mem, lat = lax.axis_index("mem"), lax.axis_index("lat")
    z, c, h, s, w = place()
    mine = w * 2 + c
    group = member(z, w, c)
    patch = group * 2 + c

    def peer(i):
        dx, dy, dc = PEERS[i - 1]
        k = ((w // 2 + dx) % 4) * 4 + ((w + dy) % 2) * 2 + (c + dc) % 2
        return k, device(z, k % 2, h, s, k // 2)

    hops = lane(w, z, c) != z
    hop_to, hop_from = device(lane(w, z, c), c, h, s, w), device(group, c, h, s, w)
    up_far, down_far = (lat == 15) & (mem != 15), (lat == 16) & (mem != 0)
    up_near, down_near = (lat < 31) & jnp.logical_not(up_far), (lat > 0) & jnp.logical_not(down_far)
    relays_up, relays_down = (lat == mem) & (lat != 15), (lat == mem + 16) & (lat != 16)
    relays = relays_up | relays_down
    low_from = (mem, jnp.where((lat == 16) & (mem != 15), mem, jnp.maximum(lat - 1, 0)))
    high_from = (mem, jnp.where((lat == 15) & (mem != 0), mem + 16, jnp.minimum(lat + 1, 31)))
    relay_from = (mem, jnp.where(relays_up, 15, 16))
    enter(
        lambda i: peer(i)[1],
        ((hops, hop_from), (lat > 0, low_from), (lat < 31, high_from), (relays, relay_from)),
        (hops, lat < 31, lat > 0, relays),
    )

    def remote(source, target, sends, recvs, i, to):
        return pltpu.make_async_remote_copy(
            source, target, sends.at[i], recvs.at[i], device_id=to, device_id_type=MESH
        )

    class Edge:
        def __init__(self, i):
            if i < 2:
                ref, ends = ((diffusivity, diffusivity_edges), (north_wind, wind_edges))[i]
                first, last = ref.at[pl.ds(0, 1)], ref.at[pl.ds(7, 1)]
                bottom, top, held = ends.at[0], ends.at[1], ends.at[2]
            else:
                part = rows(OUT, i - 2)
                first, last = field.at[pl.ds(0, 8), part], field.at[pl.ds(24, 8), part]
                bottom, top, held = low[i - 2], high[i - 2], relay[i - 2]
            above, below = (mem, jnp.minimum(lat + 1, 31)), (mem, jnp.maximum(lat - 1, 0))
            self.bottom, self.top = bottom, top
            self.ups = (
                (up_near, remote(last, bottom, up_send, low_recv, i, above)),
                (up_far, remote(last, held, up_send, relay_recv, i, (mem, mem))),
            )
            self.downs = (
                (down_near, remote(first, top, down_send, high_recv, i, below)),
                (down_far, remote(first, held, down_send, relay_recv, i, (mem, mem + 16))),
            )
            self.passes = (
                (relays_up, remote(held, bottom, relay_send, low_recv, i, (mem, 16))),
                (relays_down, remote(held, top, relay_send, high_recv, i, (mem, 15))),
            )

        def start(self, far):
            for there, copy in (self.ups[far], self.downs[far]):
                pl.when(there)(copy.start)

        def fill(self):
            @pl.when(lat == 0)
            def _():
                self.bottom[...] = jnp.zeros(self.bottom.shape, jnp.float32)

            @pl.when(lat == 31)
            def _():
                self.top[...] = jnp.zeros(self.top.shape, jnp.float32)

        def forward(self):
            for (there, copy), (_, arriving) in zip(self.passes, (self.ups[1], self.downs[1])):

                @pl.when(there)
                def _():
                    arriving.wait_recv()
                    copy.start()

        def wait(self):
            pl.when(lat > 0)(self.ups[0][1].wait_recv)
            pl.when(lat < 31)(self.downs[0][1].wait_recv)

        def end(self):
            for there, copy in self.ups + self.downs + self.passes:
                pl.when(there)(copy.wait_send)

    spread_to = device(z, c, h, s, lane(w, z, c))
    spreads = lane(w, z, c) != w
    parts = list(zip(cast, near, far)) + [
        (flags, flags_near, flags_far),
        (where, where_near, where_far),
        (values, values_near, values_out),
        (errors, errors_near, errors_out),
    ]
    spread = [Move(a, b, spread_send.at[i], spread_recv.at[i], spread_to, spreads) for i, (a, b, _) in enumerate(parts)]
    hop = [Move(b, d, hop_send.at[i], hop_recv.at[i], hop_to, hops) for i, (_, b, d) in enumerate(parts)]

    def piece(i, off):
        k, there = peer(off)
        wanted = member(z, k // 2, k % 2) * 2 + k % 2
        return pltpu.make_async_remote_copy(
            stage[i].at[wanted],
            out.at[mine, rows(OUT, i)],
            send.at[i, off],
            recv.at[i, off],
            device_id=there,
            device_id_type=MESH,
        )

    def own(i):
        return pltpu.make_async_copy(stage[i].at[patch], out.at[mine, rows(OUT, i)], recv.at[i, 0])

    def ends(i):
        column = lax.broadcasted_iota(jnp.int32, (OUT[i], 128), 1)
        return column == 0, column == 127

    def tile(k):
        return [factors[k, q : q + 1] for q in range(8)]

    def forecast(i):
        size, part = OUT[i], rows(OUT, i)
        first_lane, last_lane = ends(i)

        def before(k):
            if isinstance(k, int) and k < 2:
                return [low[i][4 * k + q] for q in range(4)]
            if isinstance(k, int) and k > 9:
                return [high[i][4 * k - 40 + q] for q in range(4)]
            return [field[4 * k - 8 + q, part] for q in range(4)]

        def middle(k):
            return [once[4 * k + q, :size] for q in range(4)]

        def first(r):
            new = advance(before(r + 1), before(r), before(r + 2), tile(r), first_lane, last_lane)
            for q in range(4):
                once[4 * r + q, :size] = new[q]

        for r in (0, 1, 8, 9):
            first(r)
        pl.loop(2, 8)(first)

        @pl.loop(0, 8)
        def _(r):
            new = advance(middle(r + 1), middle(r), middle(r + 2), tile(r + 1), first_lane, last_lane)
            for q in range(4):
                cast[i][4 * r + q] = new[q]

    def observe(i):
        tiles, put = far[i], stage[i]
        first_lane, _ = ends(i)

        @pl.loop(0, 8)
        def _(half):
            for p in range(2):
                for t in range(2):
                    put[2 * half + p, :, t * 128 : (t + 1) * 128] = tiles[4 * half + 2 * p + t]
                for j in range(4):
                    at = half * 8 + p * 4 + j
                    direct = tiles[blocks[0, at]]
                    beside = jnp.where(first_lane, tiles[blocks[1, at]], direct)
                    east = pltpu.roll(beside, 127, 1)
                    flag = averaged[half, p * 4 + j : p * 4 + j + 1]
                    seen = jnp.where(flag == 1, 0.5 * (direct + east), direct)
                    put[2 * half + p, :, 256 + j * 128 : 384 + j * 128] = seen

        for off in range(1, 16):
            piece(i, off).start()

        own(i).start()

    edges = [Edge(i) for i in range(n + 2)]
    for edge in edges:
        edge.start(1)
    for edge in edges[:3]:
        edge.start(0)
    for edge in edges:
        edge.fill()
    for edge in edges:
        edge.forward()
    for edge in edges[3:]:
        edge.start(0)
    for move in spread[n:]:
        move.start()
    for k, ref in enumerate((diffusivity, north_wind)):
        for q in range(4):
            for r in range(8):
                factors[r + 1, 4 * k + q : 4 * k + q + 1] = ref[r : r + 1, q * 128 : (q + 1) * 128]
    for k, ref in enumerate((diffusivity_edges, wind_edges)):
        edges[k].wait()
        for q in range(4):
            for at, r in ((0, 0), (1, 9)):
                factors[r, 4 * k + q : 4 * k + q + 1] = ref[at, :, q * 128 : (q + 1) * 128]
    for i in range(n):
        edges[i + 2].wait()
        forecast(i)
        spread[i].start()
        if i == 1:
            for move, after in zip(spread[n:] + spread[:1], hop[n:] + hop[:1]):
                move.wait_recv()
                after.start()
    for i in range(n):
        if i + 1 < n:
            spread[i + 1].wait_recv()
            hop[i + 1].start()
        if i == 0:
            for move in hop[n:]:
                move.wait_recv()
            for p in range(16):
                for j in range(4):
                    at = p % 2 * 4 + j
                    averaged[p // 2, at : at + 1] = flags_far[p : p + 1, j * 128 : (j + 1) * 128]
            read = pltpu.make_async_copy(where_far, blocks, table)
            read.start()
            read.wait()
        hop[i].wait_recv()
        observe(i)
    for edge in edges:
        edge.end()
    for move in spread + hop:
        move.wait_send()
    for i in range(n):

        for off in range(1, 16):
            piece(i, off).wait()

        own(i).wait()


def gather(field, diffusivity, north_wind, flags, values, errors, where):
    def buffer(*shape, dtype=jnp.float32):
        return pltpu.VMEM(shape, dtype)

    n = len(OUT)
    dma, table = pltpu.SemaphoreType.DMA, buffer(8, 128, dtype=jnp.int32)
    vmem = pl.BlockSpec(memory_space=pltpu.VMEM)
    row = jax.ShapeDtypeStruct((1, 512), jnp.float32)
    return pl.pallas_call(
        gather_kernel,
        out_shape=(jax.ShapeDtypeStruct((16, MEMBERS, 768), jnp.float32), row, row),
        in_specs=[vmem] * 7,
        out_specs=(vmem,) * 3,
        scratch_shapes=[buffer(8, size, 128) for size in OUT * 3]
        + [buffer(32, size, 128) for size in OUT * 3]
        + [buffer(16, size, 768) for size in OUT]
        + [buffer(3, 1, 512)] * 2
        + [buffer(1, 512)] * 2
        + [buffer(16, 512, dtype=jnp.int32)] * 2
        + [table, table, pltpu.SMEM((8, 128), jnp.int32), buffer(40, max(OUT), 128)]
        + [buffer(10, 8, 128), buffer(8, 8, 128, dtype=jnp.int32)]
        + [dma((n + 2,))] * 6
        + [dma((n + 4,))] * 4
        + [dma((n, 16))] * 2
        + [dma],
        compiler_params=pltpu.CompilerParams(
            collective_id=0, has_side_effects=True, vmem_limit_bytes=40 * 2**20
        ),
        name="gather",
    )(field, diffusivity, north_wind, flags, values, errors, where)


def scatter_kernel(cells, out, *scratch):
    held = scratch[:len(BACK)]
    home_send, home_recv, send, recv = scratch[len(BACK):]
    z, c, h, s, w = place()
    mine = w * 2 + c
    group = member(z, w, c)
    patch = group * 2 + c

    def peer(i):
        dx, dy, dc = PEERS[i - 1]
        k = ((w // 2 + dx) % 4) * 4 + ((w + dy) % 2) * 2 + (c + dc) % 2
        return k, device(z, k % 2, h, s, k // 2)

    home, guest = device(group, c, h, s, z), device(w, c, h, s, lane(w, z, c))
    away = jnp.logical_or(w != z, group != z)
    enter(lambda i: peer(i)[1], ((away, guest),), (away,))

    def piece(i, off):
        k, where = peer(off)
        return pltpu.make_async_remote_copy(
            cells.at[k, rows(BACK, i)],
            held[i].at[patch],
            send.at[i, off],
            recv.at[i, off],
            device_id=where,
            device_id_type=MESH,
        )

    def own(i):
        return pltpu.make_async_copy(cells.at[mine, rows(BACK, i)], held[i].at[patch], recv.at[i, 0])

    def start(i):
        for off in range(1, 16):
            piece(i, off).start()

        own(i).start()

    back = [
        Move(held[i], out.at[:, rows(BACK, i)], home_send.at[i], home_recv.at[i], home, away)
        for i in range(len(BACK))
    ]
    start(0)
    for i in range(len(BACK)):

        for off in range(1, 16):
            piece(i, off).wait_recv()

        own(i).wait()
        back[i].start()
        if i + 1 < len(BACK):
            start(i + 1)
    for i in range(len(BACK)):
        back[i].wait_recv()
        back[i].wait_send()

        for off in range(1, 16):
            piece(i, off).wait_send()


def scatter(cells):
    dma = pltpu.SemaphoreType.DMA
    vmem = pl.BlockSpec(memory_space=pltpu.VMEM)
    return pl.pallas_call(
        scatter_kernel,
        out_shape=jax.ShapeDtypeStruct((16, MEMBERS, 256), jnp.float32),
        in_specs=[vmem],
        out_specs=vmem,
        scratch_shapes=[pltpu.VMEM((16, size, 256), jnp.float32) for size in BACK]
        + [dma((len(BACK),))] * 2
        + [dma((len(BACK), 16))] * 2,
        compiler_params=pltpu.CompilerParams(
            collective_id=1, has_side_effects=True, vmem_limit_bytes=40 * 2**20
        ),
        name="scatter",
    )(cells)


def dot(left, right):
    return jnp.dot(left, right, precision=PREC, preferred_element_type=jnp.float32)


def analyse(states, values, errors):
    count = states.shape[0]
    mean = jnp.mean(states, axis=0)
    offset = states - mean
    seen_offset = offset[:, 256:]
    products = lax.dot_general(
        offset, seen_offset, (((0,), (0,)), ((), ())), precision=PREC, preferred_element_type=jnp.float32
    ) / (count - 1.0)
    covariance = products[256:] + jnp.diag(errors)
    scale = lax.rsqrt(jnp.sum(jnp.abs(covariance), axis=1))
    power = jnp.eye(512, dtype=jnp.float32) - covariance * scale[:, None] * scale[None, :]
    gain = products[:256] * scale[None, :]
    for _ in range(3):
        both_products = dot(jnp.concatenate([gain, power]), power)
        gain, power = gain + both_products[:256], both_products[256:]
    gain = (gain + dot(gain, power)) * scale[None, :]
    weights = (values - mean[256:])[None, :] - 0.5 * seen_offset
    update = lax.dot_general(
        weights, gain, (((1,), (1,)), ((), ())), precision=PREC, preferred_element_type=jnp.float32
    )
    return states[:, :256] + update


def body(ensemble, diffusivity, north_wind, observed_blocks, eastern_average_flags, observed_values, observed_error):
    blocks = observed_blocks[0].reshape(1, 64)
    nexts = blocks - blocks % 4 + (blocks + 1) % 4
    where = jnp.pad(jnp.concatenate([blocks, nexts]), ((0, 6), (0, 64)))
    field = ensemble.reshape(MEMBERS, 8, 4, 128).transpose(1, 2, 0, 3).reshape(32, MEMBERS, 128)
    states, values, errors = gather(
        field, diffusivity, north_wind, eastern_average_flags[0], observed_values[0], observed_error[0], where
    )
    states, values, errors = states.reshape(16 * MEMBERS, 768), values[0], errors[0]
    cells = analyse(states, values, errors).reshape(16, MEMBERS, 256)
    out = scatter(cells)
    return out.reshape(8, 2, MEMBERS, 256).transpose(2, 0, 1, 3).reshape(MEMBERS, 8, 512)


def solution(mesh):
    return jax.shard_map(
        body,
        mesh=mesh,
        in_specs=(
            P("mem", "lat", None),
            P("lat", None),
            P("lat", None),
            P("lat", None, None),
            P("lat", None, None),
            P("lat", "mem", None),
            P("lat", "mem", None),
        ),
        out_specs=P("mem", "lat", None),
        check_vma=False,
    )
```
